512 devices in a mesh: space: 16 (over z_lo, x), tm: 16 (over y, core), fsdp: 2 (over z_hi).
Axes of the slice: x: 4, y: 8, z: 8 (z_hi: 2, z_lo: 4; z = z_hi * 4 + z_lo), core: 2. Of those that a mesh axis runs over, the one named last changes fastest.
Arguments:
- space_query: bfloat16 [2, 32, 1024, 1024], P('fsdp', 'tm', 'space'), may hold values from -6 to 6, as said below
- space_key: bfloat16 [2, 32, 1024, 1024], P('fsdp', 'tm', 'space'), may hold values from -6 to 6, as said below
- space_value: bfloat16 [2, 32, 1024, 1024], P('fsdp', 'tm', 'space'), may hold values from -6 to 6
- time_query: bfloat16 [2, 32, 1024, 1024], P('fsdp', 'tm', 'space'), may hold values from -6 to 6, as said below
- time_key: bfloat16 [2, 32, 1024, 1024], P('fsdp', 'tm', 'space'), may hold values from -6 to 6, as said below
- stream: bfloat16 [2, 32, 1024, 1024], P('fsdp', 'tm', 'space'), may hold values from -6 to 6
- cotangent: bfloat16 [2, 32, 1024, 1024], P('fsdp', 'tm', 'space'), may hold values from -6 to 6
- mix_weight: bfloat16 [1024, 1024], P(('space', 'tm', 'fsdp')), may hold values from -0.1875 to 0.1875
Outputs:
- grad_space_query: bfloat16 [2, 32, 1024, 1024], P('fsdp', 'tm', None, 'space')
- grad_space_key: bfloat16 [2, 32, 1024, 1024], P('fsdp', 'tm', None, 'space')
- grad_space_value: bfloat16 [2, 32, 1024, 1024], P('fsdp', 'tm', None, 'space')
- grad_time_query: bfloat16 [2, 32, 1024, 1024], P('fsdp', None, ('space', 'tm'))
- grad_time_key: bfloat16 [2, 32, 1024, 1024], P('fsdp', None, ('space', 'tm'))
- grad_stream: bfloat16 [2, 32, 1024, 1024], P('fsdp', 'tm', 'space')
- grad_mix_weight: float32 [1024, 1024], P(('space', 'tm', 'fsdp'))
The draws below stay inside these ranges and needn't reach their ends.
Inputs may be any that keep to these rules, and one draw needn't show every extreme that they name: `space_query`: real-valued activations. `space_key`: real-valued activations. `time_query`: real-valued activations. `time_key`: real-valued activations.
All inputs are finite; a program needn't handle non-finite values.
Results may differ from the reference program's by a relative error of at most 0.012.
The reference program's roundings to bfloat16 on the way count: a program that leaves them out, or rounds other values in their place, can miss the bound.
Values may be sent and summed in bfloat16 or wider, within the bound.
No kernel may reach another device: no remote copies, remote signals or barrier semaphores. Data moves between devices by JAX's collectives and lax.ppermute only.
A program may use at most 64 MiB of HBM per device.

```python
import jax
import jax.numpy as jnp
from jax import lax

D = 1024
H = 16
HD = 64
B = 2
F = 32
S = 1024


def draw_space_query(key, part):
    own_key = jax.random.fold_in(key, 1)
    values = jnp.clip(jax.random.normal(own_key, (B, F, S, D), jnp.float32), -6.0, 6.0)
    return values.astype(jnp.bfloat16)


def draw_space_key(key, part):
    own_key = jax.random.fold_in(key, 2)
    values = jnp.clip(jax.random.normal(own_key, (B, F, S, D), jnp.float32), -6.0, 6.0)
    return values.astype(jnp.bfloat16)


def draw_time_query(key, part):
    own_key = jax.random.fold_in(key, 3)
    values = jnp.clip(jax.random.normal(own_key, (B, F, S, D), jnp.float32), -6.0, 6.0)
    return values.astype(jnp.bfloat16)


def draw_time_key(key, part):
    own_key = jax.random.fold_in(key, 4)
    values = jnp.clip(jax.random.normal(own_key, (B, F, S, D), jnp.float32), -6.0, 6.0)
    return values.astype(jnp.bfloat16)


def block_scale(rng, dims, cuts, low, high):
    def one(dim, blocks):
        draws = jax.random.uniform(jax.random.fold_in(jax.random.fold_in(rng, 6), dim), (blocks,), jnp.float32, low / len(cuts), high / len(cuts))
        return jnp.repeat(jnp.exp(draws), dims[dim] // blocks).reshape((-1,) + (1,) * (len(dims) - dim - 1))

    factor_of = one(*cuts[0])
    for cut in cuts[1:]:
        factor_of = factor_of * one(*cut)
    return factor_of


def scatter_about(rng, dims, deviation, most, pieces=(), kind=jnp.bfloat16):
    level = block_scale(rng, dims, pieces, -0.22, 0.18) if pieces else 1.0
    entries = jax.random.normal(rng, dims, jnp.float32) * deviation * level
    return jnp.minimum(jnp.maximum(entries, -most), most).astype(kind)


def setup_inputs(seed: int = 0) -> dict:
    streams_of = jax.random.split(jax.random.key(seed), 9)
    space_query = draw_space_query(jax.random.fold_in(streams_of[8], 71), 0)
    space_key = draw_space_key(jax.random.fold_in(streams_of[8], 71), 0)
    space_value = scatter_about(streams_of[2], (B, F, S, D), 1.0, 6.0, ((0, 2), (1, 16), (2, 16)))
    time_query = draw_time_query(jax.random.fold_in(streams_of[8], 71), 0)
    time_key = draw_time_key(jax.random.fold_in(streams_of[8], 71), 0)
    stream = scatter_about(streams_of[5], (B, F, S, D), 1.0, 6.0, ((0, 2), (1, 16), (2, 16)))
    cotangent = scatter_about(streams_of[6], (B, F, S, D), 1.0, 6.0, ((0, 2), (1, 16), (2, 16)))
    mix_weight = scatter_about(streams_of[7], (D, D), D ** -0.5, 0.1875, ((0, 512),))
    return dict(space_query=space_query, space_key=space_key, space_value=space_value, time_query=time_query, time_key=time_key, stream=stream, cotangent=cotangent, mix_weight=mix_weight)


def softmax_rows(scores):
    largest = jnp.max(scores, axis=-1, keepdims=True)
    weights = jnp.exp(scores - largest)
    return weights / jnp.sum(weights, axis=-1, keepdims=True)


def bf16_round(tensor):
    return lax.optimization_barrier(tensor.astype(jnp.bfloat16)).astype(jnp.float32)


def reference(space_query, space_key, space_value, time_query, time_key, stream, cotangent, mix_weight):
    scaling = HD ** -0.5
    query_time = time_query.reshape(B, F, S, H, HD).astype(jnp.float32)
    key_time = time_key.reshape(B, F, S, H, HD).astype(jnp.float32)
    value_time = stream.reshape(B, F, S, H, HD).astype(jnp.float32)
    grad_out = cotangent.reshape(B, F, S, H, HD).astype(jnp.float32)
    scores = jnp.einsum("bfshd,bgshd->bshfg", query_time, key_time) * scaling
    causal = lax.broadcasted_iota(jnp.int32, (F, F), 1) <= lax.broadcasted_iota(jnp.int32, (F, F), 0)
    scores = jnp.where(causal, scores, -jnp.inf)
    weights = softmax_rows(scores)
    rounded = bf16_round(weights)
    prob_grad = jnp.einsum("bfshd,bgshd->bshfg", grad_out, value_time)
    row_delta = jnp.sum(weights * prob_grad, axis=-1, keepdims=True)
    score_grad = bf16_round(weights * (prob_grad - row_delta) * scaling)
    grad_time_query = jnp.einsum("bshfg,bgshd->bfshd", score_grad, key_time).astype(jnp.bfloat16).reshape(B, F, S, D)
    grad_time_key = jnp.einsum("bshfg,bfshd->bgshd", score_grad, query_time).astype(jnp.bfloat16).reshape(B, F, S, D)
    value_term = jnp.einsum("bshfg,bfshd->bgshd", rounded, grad_out).reshape(B, F, S, D)
    grad_stream = (cotangent.astype(jnp.float32) + value_term).astype(jnp.bfloat16)

    flat_grad = grad_stream.reshape(-1, D)
    mix_grad = jnp.dot(flat_grad, mix_weight.T, preferred_element_type=jnp.float32).astype(jnp.bfloat16)

    def frame_step(operands):
        queries = operands[0].astype(jnp.float32)
        key_rows = operands[1].astype(jnp.float32)
        values = operands[2].astype(jnp.float32)
        out_grad = operands[3].astype(jnp.float32)
        frame_scores = jnp.einsum("shd,thd->hst", queries, key_rows) * scaling
        frame_weights = softmax_rows(frame_scores)
        frame_rounded = bf16_round(frame_weights)
        output = jnp.einsum("hst,thd->shd", frame_rounded, values).astype(jnp.bfloat16)
        frame_prob = jnp.einsum("shd,thd->hst", out_grad, values)
        frame_delta = jnp.sum(frame_weights * frame_prob, axis=-1, keepdims=True)
        frame_score_grad = bf16_round(frame_weights * (frame_prob - frame_delta) * scaling)
        grad_query = jnp.einsum("hst,thd->shd", frame_score_grad, key_rows).astype(jnp.bfloat16)
        grad_key = jnp.einsum("hst,shd->thd", frame_score_grad, queries).astype(jnp.bfloat16)
        grad_value = jnp.einsum("hst,shd->thd", frame_rounded, out_grad).astype(jnp.bfloat16)
        return grad_query, grad_key, grad_value, output

    def shaped(tensor):
        return tensor.reshape(B * F, S, H, HD)

    results = lax.map(frame_step, (shaped(space_query), shaped(space_key), shaped(space_value), shaped(mix_grad)))
    grad_space_query = results[0].reshape(B, F, S, D)
    grad_space_key = results[1].reshape(B, F, S, D)
    grad_space_value = results[2].reshape(B, F, S, D)
    output_all = results[3].reshape(-1, D)
    grad_mix_weight = lax.dot_general(output_all, flat_grad, (((0,), (0,)), ((), ())), preferred_element_type=jnp.float32)
    return (grad_space_query, grad_space_key, grad_space_value, grad_time_query, grad_time_key, grad_stream, grad_mix_weight)
```

```python
import jax
import jax.numpy as jnp
from jax import lax
from jax.experimental import pallas as pl
from jax.experimental.pallas import tpu as pltpu
from jax.sharding import Mesh, PartitionSpec as P

HD = 64
SCALING = HD ** (-0.5)
TM = ("y", "c")
BF = jnp.bfloat16
F32 = jnp.float32
LIMIT = 48 * 1024 * 1024
VM = pl.BlockSpec(memory_space=pltpu.VMEM)
SM = pl.BlockSpec(memory_space=pltpu.SMEM)


def call(kernel, outs, scratch=(), smem=0, n_in=1, flops=0, moved=0, name=None):
    shapes = [jax.ShapeDtypeStruct(s, d) for s, d in outs]
    return pl.pallas_call(
        kernel,
        out_shape=shapes,
        in_specs=[SM] * smem + [VM] * n_in,
        out_specs=[VM] * len(shapes),
        scratch_shapes=list(scratch),
        compiler_params=pltpu.CompilerParams(vmem_limit_bytes=LIMIT),
        cost_estimate=pl.CostEstimate(flops=flops, bytes_accessed=moved, transcendentals=0),
        name=name,
    )


def dot(a, b, dims):
    return lax.dot_general(a, b, (dims, ((), ())), preferred_element_type=F32)


def pack_time(tq, tk, st, ct, w, o):
    refs = (tq, tk, st, ct)
    for j in range(8):
        lanes = slice(128 * j, 128 * j + 128)
        wide = [[ref[f, :, lanes].astype(F32) for f in range(2)] for ref in refs]
        for g in range(16):
            rows = slice(4 * g, 4 * g + 4)
            block = jnp.concatenate([wide[a][f][rows] for a in range(4) for f in range(2)], 0)
            o[g, 32 * j : 32 * j + 32, :] = block.astype(BF)
    own = w[...].astype(F32)
    own = jnp.concatenate([own[:, 128 * j : 128 * j + 128] for j in range(8)], 0).astype(BF)
    for g in range(16):
        o[g, 256:272, :] = own


def time_grads(r, gq, gk, gs, wo):
    row = lax.broadcasted_iota(jnp.int32, (128, 128), 0)
    col = lax.broadcasted_iota(jnp.int32, (128, 128), 1)
    allowed = ((row & 3) == (col & 3)) & (row <= col)
    first = col < 64
    zero = jnp.zeros((128, 128), BF)
    kept = []
    for j in range(8):
        block = r[:, 32 * j : 32 * j + 32, :].astype(F32)
        q, k, v, g = (block[:, 8 * a : 8 * a + 8, :].reshape(128, 128).astype(BF) for a in range(4))
        sum_q = sum_k = sum_v = None
        for h in range(2):
            own = first if h == 0 else jnp.logical_not(first)
            qh, kh, gh = (jnp.where(own, t, zero) for t in (q, k, g))
            score = dot(k, qh, ((1,), (1,))) * SCALING
            score = jnp.where(allowed, score, -jnp.inf)
            e = jnp.exp(score - jnp.max(score, axis=0, keepdims=True))
            weight = e / jnp.sum(e, axis=0, keepdims=True)
            prob = dot(v, gh, ((1,), (1,)))
            delta = jnp.sum(weight * prob, axis=0, keepdims=True)
            ds = (weight * (prob - delta) * SCALING).astype(BF)
            part_k = dot(ds, qh, ((1,), (0,)))
            part_v = dot(weight.astype(BF), gh, ((1,), (0,)))
            part_q = dot(ds, kh, ((0,), (0,)))
            sum_q = part_q if h == 0 else sum_q + part_q
            sum_k = part_k if h == 0 else sum_k + part_k
            sum_v = part_v if h == 0 else sum_v + part_v
        lanes = slice(128 * j, 128 * j + 128)
        gq[:, lanes] = sum_q.astype(BF)
        gk[:, lanes] = sum_k.astype(BF)
        kept.append((g.astype(F32) + sum_v).reshape(16, 8, 128))
        if j % 2 == 1:
            gs[:, 8 * j - 8 : 8 * j + 8, :] = jnp.concatenate(kept, 1).astype(BF)
            kept = []
    rows = r[:, 256:272, :].astype(F32)
    for j in range(8):
        wo[:, 128 * j : 128 * j + 128] = jnp.concatenate(
            [rows[g, 2 * j : 2 * j + 2, :] for g in range(16)], 0
        ).astype(BF)


def unpack_stream(r, gs, wide):
    for j in range(8):
        lanes = slice(128 * j, 128 * j + 128)
        block = r[:, 8 * j : 8 * j + 8, :].astype(F32)
        for f in range(2):
            part = jnp.concatenate([block[g, 4 * f : 4 * f + 4, :] for g in range(16)], 0).astype(BF)
            gs[f, :, lanes] = part
            for m in range(4):
                wide[m, 64 * f : 64 * f + 64, lanes] = part


def pack_space(ids, q, k, v, *outs):
    z = ids[0]
    for n in range(4):
        at = pl.multiple_of(lax.rem(z + n, 4) * 256, 256)
        for a, ref in enumerate((q, k, v)):
            turned = ref[:, pl.ds(at, 256)].T
            for x in range(4):
                outs[n][x, a, :, :] = turned[64 * x : 64 * x + 64, :]


def turn_space(ids, *refs):
    ins, outs = refs[:4], refs[4:]
    x = ids[1]
    for m in range(4):
        at = lax.rem(x + m, 4)
        for n in range(4):
            outs[m][n] = ins[n][at]


def space_forward(ids, s0, s1, s2, s3, heads, stats, o0, o1, o2, o3, buf, ot):
    z, x = ids[0], ids[1]
    for m, s in enumerate((s0, s1, s2, s3)):
        for n in range(4):
            buf[lax.rem(z + 4 - n, 4) * 4 + lax.rem(x + 4 - m, 4)] = s[n]
    for a in range(3):
        for f in range(2):
            heads[a, f] = jnp.concatenate(
                [buf[i, a, :, 64 * f : 64 * f + 64] for i in range(16)], 1
            )
    for f in range(2):
        k = heads[1, f].T
        v = heads[2, f]

        def tile(t, carry):
            at = pl.ds(pl.multiple_of(t * 256, 256), 256)
            q = heads[0, f, :, at] * jnp.asarray(SCALING, BF)
            score = dot(k, q, ((1,), (0,)))
            largest = jnp.max(score, axis=0, keepdims=True)
            e = jnp.exp(score - largest)
            inverse = 1.0 / jnp.sum(e, axis=0, keepdims=True)
            stats[f, 0:1, at] = largest
            stats[f, 1:2, at] = inverse
            weight = (e * inverse).astype(BF)
            ot[t, f] = dot(v, weight, ((1,), (0,))).astype(BF)
            return carry

        lax.fori_loop(0, 4, tile, 0)
    for n, o in enumerate((o0, o1, o2, o3)):
        at = lax.rem(z + n, 4)
        for f in range(2):
            o[:, 256 * f : 256 * f + 256] = ot[at, f]


def mix_grads(g, w0, w1, w2, w3, m0, m1, m2, m3):
    for w, m in ((w0, m0), (w1, m1), (w2, m2), (w3, m3)):
        for x in range(4):
            m[:, 128 * x : 128 * x + 128] = dot(w[...], g[x], ((1,), (1,))).astype(BF)


def weight_grads(ids, g, r0, r1, r2, r3, o, buf):
    z = ids[0]
    for n, r in enumerate((r0, r1, r2, r3)):
        buf[lax.rem(z + 4 - n, 4)] = r[...]
    left = buf[...].reshape(256, 512)
    for d in range(4):
        lanes = slice(256 * d, 256 * d + 256)
        right = jnp.concatenate(
            [g[x, 64 * f : 64 * f + 64, lanes] for f in range(2) for x in range(4)], 0
        )
        total = dot(left, right, ((1,), (0,))).reshape(4, 16, 4, 256)
        for y in range(16):
            o[y, :, lanes] = jnp.concatenate([total[n, y] for n in range(4)], 0).astype(BF)


def space_backward(ids, heads, stats, m0, m1, m2, m3, gq, gk, gv, buf, got, ds_all, w_all):
    z = ids[0]
    for n, m in enumerate((m0, m1, m2, m3)):
        buf[lax.rem(z + n, 4)] = m[...]
    scale = jnp.asarray(SCALING, BF)
    for f in range(2):
        got[...] = jnp.concatenate(
            [buf[n, :, 128 * x + 64 * f : 128 * x + 64 * f + 64] for n in range(4) for x in range(4)], 1
        )
        kt = heads[1, f]
        k = kt.T
        v = heads[2, f].T
        kt = kt * scale

        def tile(t, carry):
            at = pl.ds(pl.multiple_of(t * 256, 256), 256)
            q = heads[0, f, :, at] * scale
            weight = jnp.exp(dot(k, q, ((1,), (0,))) - stats[f, 0:1, at]) * stats[f, 1:2, at]
            prob = dot(v, got[:, at], ((1,), (0,)))
            delta = jnp.sum(weight * prob, axis=0, keepdims=True)
            ds = (weight * (prob - delta)).astype(BF)
            ds_all[:, at] = ds
            w_all[:, at] = weight.astype(BF)
            gq[f, at, :] = dot(kt, ds, ((1,), (0,))).T.astype(BF)
            return carry

        lax.fori_loop(0, 4, tile, 0)
        gk[f] = dot(ds_all[...], (heads[0, f] * scale).T, ((1,), (0,))).astype(BF)
        gv[f] = dot(w_all[...], got[...].T, ((1,), (0,))).astype(BF)


def shift(value, axis, by):
    return lax.ppermute(value, axis, [(i, (i + by) % 4) for i in range(4)])


def body(space_query, space_key, space_value, time_query, time_key, stream, cotangent, mix_weight):
    ids = jnp.stack([lax.axis_index("z"), lax.axis_index("x")]).astype(jnp.int32)

    packed = call(pack_time, [((16, 272, 128), BF)], n_in=5, moved=2 << 20, name="pack_time")(
        *(t.reshape(2, 64, 1024) for t in (time_query, time_key, stream, cotangent)), mix_weight
    )[0]
    frames = lax.all_to_all(packed, TM, 0, 0, tiled=True)

    sent = call(pack_space, [((4, 3, 64, 128), BF)] * 4, smem=1, n_in=3, moved=1536 << 10, name="pack_space")(
        ids, *(t.reshape(128, 1024) for t in (space_query, space_key, space_value))
    )
    along_z = [sent[0]] + [shift(sent[n], "z", n) for n in (1, 2, 3)]
    turned = call(turn_space, [((4, 3, 64, 128), BF)] * 4, smem=1, n_in=4, moved=1536 << 10, name="turn_space")(
        ids, *along_z
    )
    along_x = [turned[0]] + [shift(turned[m], "x", m) for m in (1, 2, 3)]

    grad_time_query, grad_time_key, grad_frames, own_rows = call(
        time_grads,
        [((128, 1024), BF), ((128, 1024), BF), ((16, 64, 128), BF), ((32, 1024), BF)],
        flops=1 << 30,
        moved=2 << 20,
        name="time_grads",
    )(frames)
    back = lax.all_to_all(grad_frames, TM, 0, 0, tiled=True)

    other_rows = lax.ppermute(own_rows, "f", [(0, 1), (1, 0)])
    is_first = lax.axis_index("f") == 0
    low = jnp.where(is_first, own_rows, other_rows).reshape(16, 1, 2, 1024)
    high = jnp.where(is_first, other_rows, own_rows).reshape(16, 1, 2, 1024)
    rows = jnp.concatenate([low, high], axis=1).reshape(64, 1024)
    all_rows = [rows] + [shift(rows, "z", n) for n in (1, 2, 3)]

    heads, stats, *outputs = call(
        space_forward,
        [((3, 2, 64, 1024), BF), ((2, 2, 1024), F32)] + [((64, 512), BF)] * 4,
        scratch=[pltpu.VMEM((16, 3, 64, 128), BF), pltpu.VMEM((4, 2, 64, 256), BF)],
        smem=1,
        n_in=4,
        flops=4 << 30,
        moved=2 << 20,
        name="space_forward",
    )(ids, *along_x)
    outputs = [outputs[0]] + [shift(outputs[n], "z", n) for n in (1, 2, 3)]

    grad_stream, wide = call(
        unpack_stream, [((2, 64, 1024), BF), ((4, 128, 1024), BF)], moved=1536 << 10, name="unpack_stream"
    )(back)
    gathered = lax.all_to_all(wide, "x", 0, 0, tiled=True)

    mixed = call(
        mix_grads, [((64, 512), BF)] * 4, n_in=5, flops=1 << 28, moved=2 << 20, name="mix_grads"
    )(gathered, *all_rows)
    mixed = [mixed[0]] + [shift(mixed[n], "z", -n) for n in (1, 2, 3)]

    partial = call(
        weight_grads,
        [((16, 16, 1024), BF)],
        scratch=[pltpu.VMEM((4, 64, 512), BF)],
        smem=1,
        n_in=5,
        flops=1 << 28,
        moved=2 << 20,
        name="weight_grads",
    )(ids, gathered, *outputs)[0]
    partial = lax.all_to_all(partial, TM, 0, 0, tiled=True)

    grad_query, grad_key, grad_value = call(
        space_backward,
        [((2, 1024, 64), BF)] * 3,
        scratch=[
            pltpu.VMEM((4, 64, 512), BF),
            pltpu.VMEM((64, 1024), BF),
            pltpu.VMEM((1024, 1024), BF),
            pltpu.VMEM((1024, 1024), BF),
        ],
        smem=1,
        n_in=6,
        flops=8 << 30,
        moved=4 << 20,
        name="space_backward",
    )(ids, heads, stats, *mixed)

    partial = jnp.sum(partial.astype(F32), axis=0).reshape(8, 2, 1024)
    partial = lax.all_to_all(partial, ("z", "f"), 0, 0, tiled=True)
    grad_mix_weight = jnp.sum(partial, axis=0)

    frame_shape = (1, 2, 1024, 64)
    time_shape = (1, 32, 4, 1024)
    return (
        grad_query.reshape(frame_shape),
        grad_key.reshape(frame_shape),
        grad_value.reshape(frame_shape),
        grad_time_query.reshape(time_shape),
        grad_time_key.reshape(time_shape),
        grad_stream.reshape(1, 2, 64, 1024),
        grad_mix_weight,
    )


def solution(mesh):
    fine = Mesh(mesh.devices.reshape(4, 4, 8, 2, 2), ("z", "x", "y", "c", "f"))
    tokens = P("f", TM, ("z", "x"), None)
    feature = P("f", TM, None, ("z", "x"))
    time = P("f", None, ("z", "x", "y", "c"), None)
    rows = P(("z", "x", "y", "c", "f"), None)
    return jax.shard_map(
        body,
        mesh=fine,
        in_specs=(tokens,) * 7 + (rows,),
        out_specs=(feature,) * 3 + (time,) * 2 + (tokens, rows),
        check_vma=False,
    )
```

```python
import jax
import jax.numpy as jnp
from jax import lax
from jax.experimental import pallas as pl
from jax.experimental.pallas import tpu as pltpu
from jax.sharding import Mesh, PartitionSpec as P

HD = 64
SCALING = HD ** (-0.5)
TM = ("y", "c")
BF = jnp.bfloat16
F32 = jnp.float32
LIMIT = 48 * 1024 * 1024
WHOLE = 60 * 1024 * 1024
VM = pl.BlockSpec(memory_space=pltpu.VMEM)
SM = pl.BlockSpec(memory_space=pltpu.SMEM)
ANY = pl.BlockSpec(memory_space=pl.ANY)
HBM = pl.BlockSpec(memory_space=pltpu.HBM)


def call(kernel, outs, ins, specs=None, scratch=(), flops=0, moved=0, name=None, after=(), limit=LIMIT):
    shapes = [jax.ShapeDtypeStruct(s, d) for s, d in outs]
    specs = specs or [VM] * len(ins)
    first, count = len(ins), len(after)

    def run(*refs):
        kernel(*refs[:first], *refs[first + count :])

    return pl.pallas_call(
        run,
        out_shape=shapes,
        in_specs=list(specs) + [ANY] * count,
        out_specs=[VM] * len(shapes),
        scratch_shapes=list(scratch),
        compiler_params=pltpu.CompilerParams(vmem_limit_bytes=limit),
        cost_estimate=pl.CostEstimate(flops=flops, bytes_accessed=moved, transcendentals=0),
        name=name,
    )(*ins, *after)


def fetch(pairs, sem):
    copies = [pltpu.make_async_copy(a, b, sem.at[i]) for i, (a, b) in enumerate(pairs)]
    for copy in copies:
        copy.start()
    return copies


def dot(a, b, dims):
    return lax.dot_general(a, b, (dims, ((), ())), preferred_element_type=F32)


def pack_time(tq, tk, st, ct, w, o, buf, sem):
    pairs = [(ref.at[f], buf.at[a, f]) for a, ref in enumerate((tq, tk, st, ct)) for f in range(2)]
    for copy in fetch(pairs, sem):
        copy.wait()
    for j in range(8):
        lanes = slice(128 * j, 128 * j + 128)
        wide = [[buf[a, f, :, lanes].astype(F32) for f in range(2)] for a in range(4)]
        for g in range(16):
            rows = slice(4 * g, 4 * g + 4)
            block = jnp.concatenate([wide[a][f][rows] for a in range(4) for f in range(2)], 0)
            o[g, 32 * j : 32 * j + 32, :] = block.astype(BF)
    own = w[...].astype(F32)
    own = jnp.concatenate([own[:, 128 * j : 128 * j + 128] for j in range(8)], 0).astype(BF)
    for g in range(16):
        o[g, 256:272, :] = own


def time_grads(r, gq, gk, gs, wo):
    row = lax.broadcasted_iota(jnp.int32, (128, 128), 0)
    col = lax.broadcasted_iota(jnp.int32, (128, 128), 1)
    allowed = ((row & 3) == (col & 3)) & (row <= col)
    first = col < 64
    zero = jnp.zeros((128, 128), BF)
    kept = []
    for j in range(8):
        block = r[:, 32 * j : 32 * j + 32, :].astype(F32)
        q, k, v, g = (block[:, 8 * a : 8 * a + 8, :].reshape(128, 128).astype(BF) for a in range(4))
        sum_q = sum_k = sum_v = None
        for h in range(2):
            own = first if h == 0 else jnp.logical_not(first)
            qh, kh, gh = (jnp.where(own, t, zero) for t in (q, k, g))
            score = dot(k, qh, ((1,), (1,))) * SCALING
            score = jnp.where(allowed, score, -jnp.inf)
            e = jnp.exp(score - jnp.max(score, axis=0, keepdims=True))
            weight = e / jnp.sum(e, axis=0, keepdims=True)
            prob = dot(v, gh, ((1,), (1,)))
            delta = jnp.sum(weight * prob, axis=0, keepdims=True)
            ds = (weight * (prob - delta) * SCALING).astype(BF)
            part_k = dot(ds, qh, ((1,), (0,)))
            part_v = dot(weight.astype(BF), gh, ((1,), (0,)))
            part_q = dot(ds, kh, ((0,), (0,)))
            sum_q = part_q if h == 0 else sum_q + part_q
            sum_k = part_k if h == 0 else sum_k + part_k
            sum_v = part_v if h == 0 else sum_v + part_v
        lanes = slice(128 * j, 128 * j + 128)
        gq[:, :, lanes] = sum_q.reshape(32, 4, 128).astype(BF)
        gk[:, :, lanes] = sum_k.reshape(32, 4, 128).astype(BF)
        kept.append((g.astype(F32) + sum_v).reshape(16, 8, 128))
        if j % 2 == 1:
            gs[:, 8 * j - 8 : 8 * j + 8, :] = jnp.concatenate(kept, 1).astype(BF)
            kept = []
    rows = r[:, 256:272, :].astype(F32)
    for j in range(8):
        wo[:, 128 * j : 128 * j + 128] = jnp.concatenate(
            [rows[g, 2 * j : 2 * j + 2, :] for g in range(16)], 0
        ).astype(BF)


def unpack_stream(ids, r, own, other, s0, s1, s2, s3, gs, wide, *outs):
    for s, o in zip((s0, s1, s2, s3), outs):
        o[:, 0:512] = s[...]
    swapped = jnp.full((32, 128), ids[2], jnp.int32) == 1
    for j in range(8):
        lanes = slice(128 * j, 128 * j + 128)
        mine, theirs = own[:, lanes].astype(F32), other[:, lanes].astype(F32)
        low = jnp.where(swapped, theirs, mine)
        high = jnp.where(swapped, mine, theirs)
        pieces = [t[2 * y : 2 * y + 2] for y in range(16) for t in (low, high)]
        rows = jnp.concatenate(pieces, 0).astype(BF)
        for o in outs:
            o[:, 512 + 128 * j : 640 + 128 * j] = rows
    for j in range(8):
        lanes = slice(128 * j, 128 * j + 128)
        block = r[:, 8 * j : 8 * j + 8, :].astype(F32)
        for f in range(2):
            part = jnp.concatenate([block[g, 4 * f : 4 * f + 4, :] for g in range(16)], 0).astype(BF)
            gs[f, :, lanes] = part
            for m in range(4):
                wide[m, 64 * f : 64 * f + 64, lanes] = part


def pack_space(ids, q, k, v, o0, o1, o2, o3, buf, turned, sem):
    x = ids[1]
    copies = fetch([(ref, buf.at[a]) for a, ref in enumerate((q, k, v))], sem)
    for a in range(3):
        copies[a].wait()
        turned[...] = buf[a].T.reshape(16, 64, 128)
        for m, o in enumerate((o0, o1, o2, o3)):
            for z in range(4):
                o[z, a, :, :] = turned[z * 4 + lax.rem(x + m, 4)]


def turn_space(ids, *refs):
    ins, outs = refs[:4], refs[4:]
    z = ids[0]
    for n in range(4):
        at = lax.rem(z + n, 4)
        for m in range(4):
            outs[n][m] = ins[m][at]


def space_forward(ids, s0, s1, s2, s3, heads, stats, o0, o1, o2, o3, buf, ot):
    z, x = ids[0], ids[1]
    for n, s in enumerate((s0, s1, s2, s3)):
        for m in range(4):
            buf[lax.rem(z + 4 - n, 4) * 4 + lax.rem(x + 4 - m, 4)] = s[m]
    for a in range(3):
        for f in range(2):
            heads[a, f] = jnp.concatenate(
                [buf[i, a, :, 64 * f : 64 * f + 64] for i in range(16)], 1
            )
    for f in range(2):
        score = dot(heads[1, f].T, heads[0, f] * jnp.asarray(SCALING, BF), ((1,), (0,)))
        largest = jnp.max(score, axis=0, keepdims=True)
        e = jnp.exp(score - largest)
        inverse = 1.0 / jnp.sum(e, axis=0, keepdims=True)
        stats[f, 0:1, :] = largest
        stats[f, 1:2, :] = inverse
        result = dot(heads[2, f], (e * inverse).astype(BF), ((1,), (0,))).astype(BF)
        for n in range(4):
            ot[n, f] = result[:, 256 * n : 256 * n + 256]
    for n, o in enumerate((o0, o1, o2, o3)):
        at = lax.rem(z + n, 4)
        for f in range(2):
            o[:, 256 * f : 256 * f + 256] = ot[at, f]


def mix_grads(g, r0, r1, r2, r3, m0, m1, m2, m3):
    for r, m in ((r0, m0), (r1, m1), (r2, m2), (r3, m3)):
        w = r[:, 512:1536]
        for x in range(4):
            m[:, 128 * x : 128 * x + 128] = dot(w, g[x], ((1,), (1,))).astype(BF)


def weight_grads(ids, g, r0, r1, r2, r3, o, buf):
    z = ids[0]
    for n, r in enumerate((r0, r1, r2, r3)):
        buf[lax.rem(z + 4 - n, 4)] = r[:, 0:512]
    left = buf[...].reshape(256, 512)
    for d in range(4):
        lanes = slice(256 * d, 256 * d + 256)
        right = jnp.concatenate(
            [g[x, 64 * f : 64 * f + 64, lanes] for f in range(2) for x in range(4)], 0
        )
        total = dot(left, right, ((1,), (0,))).reshape(4, 16, 4, 256)
        for y in range(16):
            o[y, :, lanes] = jnp.concatenate([total[n, y] for n in range(4)], 0).astype(BF)


def space_backward(ids, heads, stats, m0, m1, m2, m3, gq, gk, gv, buf, got, ds_all, w_all):
    z = ids[0]
    for n, m in enumerate((m0, m1, m2, m3)):
        buf[lax.rem(z + n, 4)] = m[...]
    scale = jnp.asarray(SCALING, BF)
    for f in range(2):
        got[...] = jnp.concatenate(
            [buf[n, :, 128 * x + 64 * f : 128 * x + 64 * f + 64] for n in range(4) for x in range(4)], 1
        )
        q, k = heads[0, f] * scale, heads[1, f]
        weight = jnp.exp(dot(k.T, q, ((1,), (0,))) - stats[f, 0:1, :]) * stats[f, 1:2, :]
        prob = dot(heads[2, f].T, got[...], ((1,), (0,)))
        delta = jnp.sum(weight * prob, axis=0, keepdims=True)
        ds_all[...] = (weight * (prob - delta)).astype(BF)
        w_all[...] = weight.astype(BF)
        gq[f] = dot(k * scale, ds_all[...], ((1,), (0,))).astype(BF)
        gk[f] = dot(ds_all[...], q.T, ((1,), (0,))).T.astype(BF)
        gv[f] = dot(w_all[...], got[...].T, ((1,), (0,))).T.astype(BF)


def add_up(r, o):
    total = r[0].astype(F32)
    for i in range(1, 16):
        total = total + r[i].astype(F32)
    for i in range(8):
        o[i] = total[2 * i : 2 * i + 2]


def shift(value, axis, by):
    return lax.ppermute(value, axis, [(i, (i + by) % 4) for i in range(4)])


def body(space_query, space_key, space_value, time_query, time_key, stream, cotangent, mix_weight):
    ids = jnp.stack([lax.axis_index(a) for a in ("z", "x", "f")]).astype(jnp.int32)

    packed = call(
        pack_time,
        [((16, 272, 128), BF)],
        [t.reshape(2, 64, 1024) for t in (time_query, time_key, stream, cotangent)] + [mix_weight],
        specs=[HBM] * 4 + [VM],
        scratch=[pltpu.VMEM((4, 2, 64, 1024), BF), pltpu.SemaphoreType.DMA((8,))],
        moved=2 << 20,
        name="pack_time",
        limit=WHOLE,
    )[0]
    frames = lax.all_to_all(packed, TM, 0, 0, tiled=True)

    part = ((4, 3, 64, 128), BF)
    sent = call(
        pack_space,
        [part] * 4,
        [ids] + [t.reshape(128, 1024) for t in (space_query, space_key, space_value)],
        specs=[SM] + [HBM] * 3,
        scratch=[
            pltpu.VMEM((3, 128, 1024), BF),
            pltpu.VMEM((16, 64, 128), BF),
            pltpu.SemaphoreType.DMA((3,)),
        ],
        moved=1536 << 10,
        name="pack_space",
        after=[packed],
    )
    along_x = [sent[0]] + [shift(sent[m], "x", m) for m in (1, 2, 3)]
    turned = call(
        turn_space, [part] * 4, [ids] + along_x, specs=[SM] + [VM] * 4, moved=1536 << 10, name="turn_space"
    )
    along_z = [turned[0]] + [shift(turned[n], "z", n) for n in (1, 2, 3)]

    grad_time_query, grad_time_key, grad_frames, own_rows = call(
        time_grads,
        [((32, 4, 1024), BF), ((32, 4, 1024), BF), ((16, 64, 128), BF), ((32, 1024), BF)],
        [frames],
        flops=1 << 30,
        moved=2 << 20,
        name="time_grads",
        after=[turned[0]],
    )
    back = lax.all_to_all(grad_frames, TM, 0, 0, tiled=True)
    other_rows = lax.ppermute(own_rows, "f", [(0, 1), (1, 0)])

    heads, stats, *outputs = call(
        space_forward,
        [((3, 2, 64, 1024), BF), ((2, 2, 1024), F32)] + [((64, 512), BF)] * 4,
        [ids] + along_z,
        specs=[SM] + [VM] * 4,
        scratch=[pltpu.VMEM((16, 3, 64, 128), BF), pltpu.VMEM((4, 2, 64, 256), BF)],
        flops=4 << 30,
        moved=2 << 20,
        name="space_forward",
    )

    grad_stream, wide, *outputs = call(
        unpack_stream,
        [((2, 64, 1024), BF), ((4, 128, 1024), BF)] + [((64, 1536), BF)] * 4,
        [ids, back, own_rows, other_rows] + outputs,
        specs=[SM] + [VM] * 7,
        moved=1536 << 10,
        name="unpack_stream",
    )
    gathered = lax.all_to_all(wide, "x", 0, 0, tiled=True)
    outputs = [outputs[0]] + [shift(outputs[n], "z", n) for n in (1, 2, 3)]

    partial = call(
        weight_grads,
        [((16, 16, 1024), BF)],
        [ids, gathered] + outputs,
        specs=[SM] + [VM] * 5,
        scratch=[pltpu.VMEM((4, 64, 512), BF)],
        flops=1 << 28,
        moved=2 << 20,
        name="weight_grads",
    )[0]
    spread = lax.all_to_all(partial, TM, 0, 0, tiled=True)
    mixed = call(
        mix_grads,
        [((64, 512), BF)] * 4,
        [gathered] + outputs,
        flops=1 << 28,
        moved=2 << 20,
        name="mix_grads",
        after=[partial],
    )
    mixed = [mixed[0]] + [shift(mixed[n], "z", -n) for n in (1, 2, 3)]

    summed = call(add_up, [((8, 2, 1024), F32)], [spread], moved=1 << 19, name="add_up", after=mixed[1:])[0]
    last = lax.all_to_all(summed, ("z", "f"), 0, 0, tiled=True)
    grads = call(
        space_backward,
        [((2, 64, 1024), BF)] * 3,
        [ids, heads, stats] + mixed,
        specs=[SM] + [VM] * 6,
        scratch=[
            pltpu.VMEM((4, 64, 512), BF),
            pltpu.VMEM((64, 1024), BF),
            pltpu.VMEM((1024, 1024), BF),
            pltpu.VMEM((1024, 1024), BF),
        ],
        flops=8 << 30,
        moved=4 << 20,
        name="space_backward",
        after=[summed],
    )
    grad_mix_weight = jnp.sum(last, axis=0)

    time_shape = (1, 32, 4, 1024)
    return (
        *(g.transpose(0, 2, 1).reshape(1, 2, 1024, 64) for g in grads),
        grad_time_query.reshape(time_shape),
        grad_time_key.reshape(time_shape),
        grad_stream.reshape(1, 2, 64, 1024),
        grad_mix_weight,
    )


def solution(mesh):
    fine = Mesh(mesh.devices.reshape(4, 4, 8, 2, 2), ("z", "x", "y", "c", "f"))
    tokens = P("f", TM, ("z", "x"), None)
    feature = P("f", TM, None, ("z", "x"))
    time = P("f", None, ("z", "x", "y", "c"), None)
    rows = P(("z", "x", "y", "c", "f"), None)
    return jax.shard_map(
        body,
        mesh=fine,
        in_specs=(tokens,) * 7 + (rows,),
        out_specs=(feature,) * 3 + (time,) * 2 + (tokens, rows),
        check_vma=False,
    )
```

```python
import jax
import jax.numpy as jnp
from jax import lax
from jax.experimental import pallas as pl
from jax.experimental.pallas import tpu as pltpu
from jax.sharding import Mesh, PartitionSpec as P

HD = 64
SCALING = HD ** (-0.5)
TM = ("y", "c")
BF = jnp.bfloat16
F32 = jnp.float32
LIMIT = 16 * 1024 * 1024
FRAME = 32 * 1024 * 1024
WHOLE = 60 * 1024 * 1024
VM = pl.BlockSpec(memory_space=pltpu.VMEM)
SM = pl.BlockSpec(memory_space=pltpu.SMEM)
ANY = pl.BlockSpec(memory_space=pl.ANY)
HBM = pl.BlockSpec(memory_space=pltpu.HBM)


def call(kernel, outs, ins, specs=None, scratch=(), flops=0, moved=0, name=None, after=(), limit=LIMIT):
    shapes = [jax.ShapeDtypeStruct(s, d) for s, d in outs]
    specs = specs or [VM] * len(ins)
    first, count = len(ins), len(after)

    def run(*refs):
        kernel(*refs[:first], *refs[first + count :])

    return pl.pallas_call(
        run,
        out_shape=shapes,
        in_specs=list(specs) + [ANY] * count,
        out_specs=[VM] * len(shapes),
        scratch_shapes=list(scratch),
        compiler_params=pltpu.CompilerParams(vmem_limit_bytes=limit),
        cost_estimate=pl.CostEstimate(flops=flops, bytes_accessed=moved, transcendentals=0),
        name=name,
    )(*ins, *after)


def fetch(pairs, sem):
    copies = [pltpu.make_async_copy(a, b, sem.at[i]) for i, (a, b) in enumerate(pairs)]
    for copy in copies:
        copy.start()
    return copies


def dot(a, b, dims):
    return lax.dot_general(a, b, (dims, ((), ())), preferred_element_type=F32)


def pack_time(tq, tk, st, ct, w, o, buf, sem):
    pairs = [(ref.at[f], buf.at[a, f]) for a, ref in enumerate((tq, tk, st, ct)) for f in range(2)]
    for copy in fetch(pairs, sem):
        copy.wait()
    for j in range(8):
        lanes = slice(128 * j, 128 * j + 128)
        wide = [[buf[a, f, :, lanes].astype(F32) for f in range(2)] for a in range(4)]
        for g in range(16):
            rows = slice(4 * g, 4 * g + 4)
            block = jnp.concatenate([wide[a][f][rows] for a in range(4) for f in range(2)], 0)
            o[g, 32 * j : 32 * j + 32, :] = block.astype(BF)
    own = w[...].astype(F32)
    own = jnp.concatenate([own[:, 128 * j : 128 * j + 128] for j in range(8)], 0).astype(BF)
    for g in range(16):
        o[g, 256:272, :] = own


def time_grads(r, gq, gk, gs, wo):
    row = lax.broadcasted_iota(jnp.int32, (128, 128), 0)
    col = lax.broadcasted_iota(jnp.int32, (128, 128), 1)
    allowed = ((row & 3) == (col & 3)) & (row <= col)
    bias = jnp.where(allowed, 0.0, -jnp.inf).astype(F32)
    zero = jnp.zeros((128, 128), BF)
    scale = jnp.asarray(SCALING, BF)
    cots, heads = [], []
    for j in range(8):
        block = r[:, 32 * j : 32 * j + 32, :].astype(F32)
        q, k, v, cot = (block[:, 8 * a : 8 * a + 8, :].reshape(128, 128) for a in range(4))
        cots.append(cot)
        q, k, v, g = (t.astype(BF) for t in (q, k, v, cot))
        for own in (col < 64, col >= 64):
            qh, kh, gh = (jnp.where(own, t, zero) for t in (q, k, g))
            heads.append((qh, k, kh, v, gh))
    scores = [dot(k, qh * scale, ((1,), (1,))) + bias for qh, k, _, _, _ in heads]
    probs = [dot(v, gh, ((1,), (1,))) for _, _, _, v, gh in heads]
    exps = [jnp.exp(s - jnp.max(s, axis=0, keepdims=True)) for s in scores]
    weights = [e * (1.0 / jnp.sum(e, axis=0, keepdims=True)) for e in exps]
    parts_v = [dot(w.astype(BF), h[4], ((1,), (0,))) for w, h in zip(weights, heads)]
    deltas = [jnp.sum(w * p, axis=0, keepdims=True) for w, p in zip(weights, probs)]
    ds = [(w * (p - d) * SCALING).astype(BF) for w, p, d in zip(weights, probs, deltas)]
    parts_k = [dot(d, h[0], ((1,), (0,))) for d, h in zip(ds, heads)]
    parts_q = [dot(d, h[2], ((0,), (0,))) for d, h in zip(ds, heads)]
    kept = []
    for j in range(8):
        lanes = slice(128 * j, 128 * j + 128)
        gq[:, :, lanes] = (parts_q[2 * j] + parts_q[2 * j + 1]).reshape(32, 4, 128).astype(BF)
        gk[:, :, lanes] = (parts_k[2 * j] + parts_k[2 * j + 1]).reshape(32, 4, 128).astype(BF)
        kept.append((cots[j] + (parts_v[2 * j] + parts_v[2 * j + 1])).reshape(16, 8, 128))
        if j % 2 == 1:
            gs[:, 8 * j - 8 : 8 * j + 8, :] = jnp.concatenate(kept, 1).astype(BF)
            kept = []
    rows = r[:, 256:272, :].astype(F32)
    for j in range(8):
        wo[:, 128 * j : 128 * j + 128] = jnp.concatenate(
            [rows[g, 2 * j : 2 * j + 2, :] for g in range(16)], 0
        ).astype(BF)


def unpack_stream(ids, r, own, other, s0, s1, s2, s3, gs, wide, *outs):
    for s, o in zip((s0, s1, s2, s3), outs):
        o[:, 0:512] = s[...]
    swapped = jnp.full((32, 128), ids[2], jnp.int32) == 1
    for j in range(4):
        lanes = pl.ds(pl.multiple_of(ids[3] * 512 + 128 * j, 128), 128)
        mine, theirs = own[:, lanes].astype(F32), other[:, lanes].astype(F32)
        low = jnp.where(swapped, theirs, mine)
        high = jnp.where(swapped, mine, theirs)
        pieces = [t[2 * y : 2 * y + 2] for y in range(16) for t in (low, high)]
        rows = jnp.concatenate(pieces, 0).astype(BF)
        for o in outs:
            o[:, 512 + 128 * j : 640 + 128 * j] = rows
    for j in range(8):
        lanes = slice(128 * j, 128 * j + 128)
        block = r[:, 8 * j : 8 * j + 8, :].astype(F32)
        for f in range(2):
            part = jnp.concatenate([block[g, 4 * f : 4 * f + 4, :] for g in range(16)], 0).astype(BF)
            gs[f, :, lanes] = part
            for m in range(4):
                wide[m, 64 * f : 64 * f + 64, lanes] = part


def pack_space(ids, q, k, v, o0, o1, o2, o3, buf, turned, sem):
    x = ids[1]
    copies = fetch([(ref, buf.at[a]) for a, ref in enumerate((q, k, v))], sem)
    for a in range(3):
        copies[a].wait()
        turned[...] = buf[a].T.reshape(16, 64, 128)
        for m, o in enumerate((o0, o1, o2, o3)):
            for z in range(4):
                o[z, a, :, :] = turned[z * 4 + lax.rem(x + m, 4)]


def turn_space(ids, *refs):
    ins, outs = refs[:4], refs[4:]
    z = ids[0]
    for n in range(4):
        at = lax.rem(z + n, 4)
        for m in range(4):
            outs[n][m] = ins[m][at]


def space_forward(ids, s0, s1, s2, s3, heads, stats, o0, o1, o2, o3, buf, ot):
    z, x = ids[0], ids[1]
    for n, s in enumerate((s0, s1, s2, s3)):
        for m in range(4):
            buf[lax.rem(z + 4 - n, 4) * 4 + lax.rem(x + 4 - m, 4)] = s[m]
    for a in range(3):
        for f in range(2):
            heads[a, f] = jnp.concatenate(
                [buf[i, a, :, 64 * f : 64 * f + 64] for i in range(16)], 1
            )
    for f in range(2):
        score = dot(heads[1, f].T, heads[0, f] * jnp.asarray(SCALING, BF), ((1,), (0,)))
        largest = jnp.max(score, axis=0, keepdims=True)
        e = jnp.exp(score - largest)
        inverse = 1.0 / jnp.sum(e, axis=0, keepdims=True)
        stats[f, 0:1, :] = largest
        stats[f, 1:2, :] = inverse
        result = dot(heads[2, f], (e * inverse).astype(BF), ((1,), (0,))).astype(BF)
        for n in range(4):
            ot[n, f] = result[:, 256 * n : 256 * n + 256]
    for n, o in enumerate((o0, o1, o2, o3)):
        at = lax.rem(z + n, 4)
        for f in range(2):
            o[:, 256 * f : 256 * f + 256] = ot[at, f]


def mix_grads(ids, g, own, other, m0, m1, m2, m3, buf):
    buf[ids[3]] = own[...]
    buf[1 - ids[3]] = other[...]
    for n, m in enumerate((m0, m1, m2, m3)):
        w = jnp.concatenate([buf[0, n], buf[1, n]], 1)
        for x in range(4):
            m[:, 128 * x : 128 * x + 128] = dot(w, g[x], ((1,), (1,))).astype(BF)


def weight_grads(ids, g, r0, r1, r2, r3, o, held, buf):
    z = ids[0]
    for n, r in enumerate((r0, r1, r2, r3)):
        held[n] = r[:, 512:1024]
    for n, r in enumerate((r0, r1, r2, r3)):
        buf[lax.rem(z + 4 - n, 4)] = r[:, 0:512]
    left = buf[...].reshape(256, 512)
    for d in range(4):
        lanes = slice(256 * d, 256 * d + 256)
        right = jnp.concatenate(
            [g[x, 64 * f : 64 * f + 64, lanes] for f in range(2) for x in range(4)], 0
        )
        total = dot(left, right, ((1,), (0,))).reshape(4, 16, 4, 256)
        for y in range(16):
            o[y, :, lanes] = jnp.concatenate([total[n, y] for n in range(4)], 0).astype(BF)


def space_backward(ids, heads, stats, m0, m1, m2, m3, gq, gk, gv, buf, got, ds_all, w_all):
    z = ids[0]
    for n, m in enumerate((m0, m1, m2, m3)):
        buf[lax.rem(z + n, 4)] = m[...]
    scale = jnp.asarray(SCALING, BF)
    for f in range(2):
        got[...] = jnp.concatenate(
            [buf[n, :, 128 * x + 64 * f : 128 * x + 64 * f + 64] for n in range(4) for x in range(4)], 1
        )
        q, k = heads[0, f] * scale, heads[1, f]
        weight = jnp.exp(dot(k.T, q, ((1,), (0,))) - stats[f, 0:1, :]) * stats[f, 1:2, :]
        prob = dot(heads[2, f].T, got[...], ((1,), (0,)))
        delta = jnp.sum(weight * prob, axis=0, keepdims=True)
        ds_all[...] = (weight * (prob - delta)).astype(BF)
        w_all[...] = weight.astype(BF)
        gq[f] = dot(k * scale, ds_all[...], ((1,), (0,))).astype(BF)
        gk[f] = dot(ds_all[...], q.T, ((1,), (0,))).T.astype(BF)
        gv[f] = dot(w_all[...], got[...].T, ((1,), (0,))).T.astype(BF)


def add_up(r, o):
    total = r[0].astype(F32)
    for i in range(1, 16):
        total = total + r[i].astype(F32)
    for i in range(8):
        o[i] = total[2 * i : 2 * i + 2]


def shift(value, axis, by):
    return lax.ppermute(value, axis, [(i, (i + by) % 4) for i in range(4)])


def body(space_query, space_key, space_value, time_query, time_key, stream, cotangent, mix_weight):
    ids = jnp.stack([lax.axis_index(a) for a in ("z", "x", "f", "c")]).astype(jnp.int32)

    packed = call(
        pack_time,
        [((16, 272, 128), BF)],
        [t.reshape(2, 64, 1024) for t in (time_query, time_key, stream, cotangent)] + [mix_weight],
        specs=[HBM] * 4 + [VM],
        scratch=[pltpu.VMEM((4, 2, 64, 1024), BF), pltpu.SemaphoreType.DMA((8,))],
        moved=2 << 20,
        name="pack_time",
        limit=WHOLE,
    )[0]
    frames = lax.all_to_all(packed, TM, 0, 0, tiled=True)

    part = ((4, 3, 64, 128), BF)
    sent = call(
        pack_space,
        [part] * 4,
        [ids] + [t.reshape(128, 1024) for t in (space_query, space_key, space_value)],
        specs=[SM] + [HBM] * 3,
        scratch=[
            pltpu.VMEM((3, 128, 1024), BF),
            pltpu.VMEM((16, 64, 128), BF),
            pltpu.SemaphoreType.DMA((3,)),
        ],
        moved=1536 << 10,
        name="pack_space",
        after=[packed],
    )
    along_x = [sent[0]] + [shift(sent[m], "x", m) for m in (1, 2, 3)]
    turned = call(
        turn_space, [part] * 4, [ids] + along_x, specs=[SM] + [VM] * 4, moved=1536 << 10, name="turn_space"
    )
    along_z = [turned[0]] + [shift(turned[n], "z", n) for n in (1, 2, 3)]

    grad_time_query, grad_time_key, grad_frames, own_rows = call(
        time_grads,
        [((32, 4, 1024), BF), ((32, 4, 1024), BF), ((16, 64, 128), BF), ((32, 1024), BF)],
        [frames],
        flops=1 << 30,
        moved=2 << 20,
        name="time_grads",
        after=[turned[0]],
    )
    back = lax.all_to_all(grad_frames, TM, 0, 0, tiled=True)
    other_rows = lax.ppermute(own_rows, "f", [(0, 1), (1, 0)])

    heads, stats, *outputs = call(
        space_forward,
        [((3, 2, 64, 1024), BF), ((2, 2, 1024), F32)] + [((64, 512), BF)] * 4,
        [ids] + along_z,
        specs=[SM] + [VM] * 4,
        scratch=[pltpu.VMEM((16, 3, 64, 128), BF), pltpu.VMEM((4, 2, 64, 256), BF)],
        flops=4 << 30,
        moved=2 << 20,
        name="space_forward",
        limit=FRAME,
    )

    grad_stream, wide, *outputs = call(
        unpack_stream,
        [((2, 64, 1024), BF), ((4, 128, 1024), BF)] + [((64, 1024), BF)] * 4,
        [ids, back, own_rows, other_rows] + outputs,
        specs=[SM] + [VM] * 7,
        moved=1536 << 10,
        name="unpack_stream",
    )
    gathered = lax.all_to_all(wide, "x", 0, 0, tiled=True)
    outputs = [outputs[0]] + [shift(outputs[n], "z", n) for n in (1, 2, 3)]

    partial, own_lanes = call(
        weight_grads,
        [((16, 16, 1024), BF), ((4, 64, 512), BF)],
        [ids, gathered] + outputs,
        specs=[SM] + [VM] * 5,
        scratch=[pltpu.VMEM((4, 64, 512), BF)],
        flops=1 << 28,
        moved=2 << 20,
        name="weight_grads",
    )
    other_lanes = lax.ppermute(own_lanes, "c", [(0, 1), (1, 0)])
    spread = lax.all_to_all(partial, TM, 0, 0, tiled=True)
    mixed = call(
        mix_grads,
        [((64, 512), BF)] * 4,
        [ids, gathered, own_lanes, other_lanes],
        specs=[SM] + [VM] * 3,
        scratch=[pltpu.VMEM((2, 4, 64, 512), BF)],
        flops=1 << 28,
        moved=2 << 20,
        name="mix_grads",
    )
    mixed = [mixed[0]] + [shift(mixed[n], "z", -n) for n in (1, 2, 3)]

    summed = call(add_up, [((8, 2, 1024), F32)], [spread], moved=1 << 19, name="add_up", after=mixed[:1])[0]
    last = lax.all_to_all(summed, ("z", "f"), 0, 0, tiled=True)
    grads = call(
        space_backward,
        [((2, 64, 1024), BF)] * 3,
        [ids, heads, stats] + mixed,
        specs=[SM] + [VM] * 6,
        scratch=[
            pltpu.VMEM((4, 64, 512), BF),
            pltpu.VMEM((64, 1024), BF),
            pltpu.VMEM((1024, 1024), BF),
            pltpu.VMEM((1024, 1024), BF),
        ],
        flops=8 << 30,
        moved=4 << 20,
        name="space_backward",
        limit=FRAME,
        after=[summed],
    )
    grad_mix_weight = jnp.sum(last, axis=0)

    time_shape = (1, 32, 4, 1024)
    return (
        *(g.transpose(0, 2, 1).reshape(1, 2, 1024, 64) for g in grads),
        grad_time_query.reshape(time_shape),
        grad_time_key.reshape(time_shape),
        grad_stream.reshape(1, 2, 64, 1024),
        grad_mix_weight,
    )


def solution(mesh):
    fine = Mesh(mesh.devices.reshape(4, 4, 8, 2, 2), ("z", "x", "y", "c", "f"))
    tokens = P("f", TM, ("z", "x"), None)
    feature = P("f", TM, None, ("z", "x"))
    time = P("f", None, ("z", "x", "y", "c"), None)
    rows = P(("z", "x", "y", "c", "f"), None)
    return jax.shard_map(
        body,
        mesh=fine,
        in_specs=(tokens,) * 7 + (rows,),
        out_specs=(feature,) * 3 + (time,) * 2 + (tokens, rows),
        check_vma=False,
    )
```

```python
import jax
import jax.numpy as jnp
from jax import lax
from jax.experimental import pallas as pl
from jax.experimental.pallas import tpu as pltpu
from jax.sharding import Mesh, PartitionSpec as P

HD = 64
SCALING = HD ** (-0.5)
TM = ("y", "c")
BF = jnp.bfloat16
F32 = jnp.float32
LIMIT = 16 * 1024 * 1024
FRAME = 32 * 1024 * 1024
WHOLE = 60 * 1024 * 1024
VM = pl.BlockSpec(memory_space=pltpu.VMEM)
SM = pl.BlockSpec(memory_space=pltpu.SMEM)
ANY = pl.BlockSpec(memory_space=pl.ANY)
HBM = pl.BlockSpec(memory_space=pltpu.HBM)


def call(kernel, outs, ins, specs=None, scratch=(), flops=0, moved=0, name=None, after=(), limit=LIMIT, places=None):
    shapes = [jax.ShapeDtypeStruct(s, d) for s, d in outs]
    specs = specs or [VM] * len(ins)
    first, count = len(ins), len(after)

    def run(*refs):
        kernel(*refs[:first], *refs[first + count :])

    return pl.pallas_call(
        run,
        out_shape=shapes,
        in_specs=list(specs) + [ANY] * count,
        out_specs=places or [VM] * len(shapes),
        scratch_shapes=list(scratch),
        compiler_params=pltpu.CompilerParams(vmem_limit_bytes=limit),
        cost_estimate=pl.CostEstimate(flops=flops, bytes_accessed=moved, transcendentals=0),
        name=name,
    )(*ins, *after)


def fetch(pairs, sem):
    copies = [pltpu.make_async_copy(a, b, sem.at[i]) for i, (a, b) in enumerate(pairs)]
    for copy in copies:
        copy.start()
    return copies


def dot(a, b, dims):
    return lax.dot_general(a, b, (dims, ((), ())), preferred_element_type=F32)


def pack_time(tq, tk, st, ct, w, o, buf, stage, sem, out_sem):
    copies = [
        pltpu.make_async_copy(
            ref.at[f, pl.ds(16 * h, 16)], buf.at[a, f, pl.ds(16 * h, 16)], sem.at[8 * h + 2 * a + f]
        )
        for h in range(4)
        for a, ref in enumerate((tq, tk, st, ct))
        for f in range(2)
    ]
    for copy in copies:
        copy.start()
    own = w[...].astype(F32)
    own = jnp.concatenate([own[:, 128 * j : 128 * j + 128] for j in range(8)], 0).astype(BF)
    for g in range(16):
        stage[g, 256:272, :] = own
    results = []
    for h in range(4):
        for copy in copies[8 * h : 8 * h + 8]:
            copy.wait()
        for j in range(8):
            lanes = slice(128 * j, 128 * j + 128)
            wide = [[buf[a, f, 16 * h : 16 * h + 16, lanes].astype(F32) for f in range(2)] for a in range(4)]
            for g in range(4):
                rows = slice(4 * g, 4 * g + 4)
                block = jnp.concatenate([wide[a][f][rows] for a in range(4) for f in range(2)], 0)
                stage[4 * h + g, 32 * j : 32 * j + 32, :] = block.astype(BF)
        results.append(
            pltpu.make_async_copy(stage.at[pl.ds(4 * h, 4)], o.at[pl.ds(4 * h, 4)], out_sem.at[h])
        )
        results[-1].start()
    for copy in results:
        copy.wait()


def time_heads(r):
    row = lax.broadcasted_iota(jnp.int32, (128, 128), 0)
    col = lax.broadcasted_iota(jnp.int32, (128, 128), 1)
    allowed = ((row & 3) == (col & 3)) & (row <= col)
    bias = jnp.where(allowed, 0.0, -jnp.inf).astype(F32)
    zero = jnp.zeros((128, 128), BF)
    scale = jnp.asarray(SCALING, BF)
    cots, heads = [], []
    for j in range(8):
        block = r[:, 32 * j : 32 * j + 32, :].astype(F32)
        q, k, v, cot = (block[:, 8 * a : 8 * a + 8, :].reshape(128, 128) for a in range(4))
        cots.append(cot)
        q, k, v, g = (t.astype(BF) for t in (q, k, v, cot))
        for own in (col < 64, col >= 64):
            qh, kh, gh = (jnp.where(own, t, zero) for t in (q, k, g))
            heads.append((qh, k, kh, v, gh))
    scores = [dot(k, qh * scale, ((1,), (1,))) + bias for qh, k, _, _, _ in heads]
    exps = [jnp.exp(s - jnp.max(s, axis=0, keepdims=True)) for s in scores]
    weights = [e * (1.0 / jnp.sum(e, axis=0, keepdims=True)) for e in exps]
    return cots, heads, weights


def time_stream(ids, r, gs, wo):
    cots, heads, weights = time_heads(r)
    parts = [dot(w.astype(BF), h[4], ((1,), (0,))) for w, h in zip(weights, heads)]
    for j in range(0, 8, 2):
        pair = [(cots[i] + (parts[2 * i] + parts[2 * i + 1])).reshape(16, 8, 128) for i in (j, j + 1)]
        gs[:, 8 * j : 8 * j + 16, :] = jnp.concatenate(pair, 1).astype(BF)
    rows = r[:, 256:272, :].astype(F32)
    rows = jnp.where(jnp.full((16, 8, 128), ids[3], jnp.int32) == 1, rows[:, 8:16], rows[:, 0:8])
    for j in range(4):
        wo[:, 128 * j : 128 * j + 128] = jnp.concatenate(
            [rows[g, 2 * j : 2 * j + 2, :] for g in range(16)], 0
        ).astype(BF)


def time_grads(r, gq, gk, token):
    token[...] = jnp.zeros((8, 128), F32)
    _, heads, weights = time_heads(r)
    probs = [dot(v, gh, ((1,), (1,))) for _, _, _, v, gh in heads]
    deltas = [jnp.sum(w * p, axis=0, keepdims=True) for w, p in zip(weights, probs)]
    ds = [(w * (p - d) * SCALING).astype(BF) for w, p, d in zip(weights, probs, deltas)]
    parts_k = [dot(d, h[0], ((1,), (0,))) for d, h in zip(ds, heads)]
    parts_q = [dot(d, h[2], ((0,), (0,))) for d, h in zip(ds, heads)]
    for j in range(8):
        lanes = slice(128 * j, 128 * j + 128)
        gq[:, :, lanes] = (parts_q[2 * j] + parts_q[2 * j + 1]).reshape(32, 4, 128).astype(BF)
        gk[:, :, lanes] = (parts_k[2 * j] + parts_k[2 * j + 1]).reshape(32, 4, 128).astype(BF)


def unpack_stream(ids, r, own, other, s0, s1, s2, s3, gs, wide, *outs):
    for s, o in zip((s0, s1, s2, s3), outs):
        o[:, 0:512] = s[...]
    swapped = jnp.full((32, 128), ids[2], jnp.int32) == 1
    for j in range(4):
        lanes = slice(128 * j, 128 * j + 128)
        mine, theirs = own[:, lanes].astype(F32), other[:, lanes].astype(F32)
        low = jnp.where(swapped, theirs, mine)
        high = jnp.where(swapped, mine, theirs)
        pieces = [t[2 * y : 2 * y + 2] for y in range(16) for t in (low, high)]
        rows = jnp.concatenate(pieces, 0).astype(BF)
        for o in outs:
            o[:, 512 + 128 * j : 640 + 128 * j] = rows
    for j in range(8):
        lanes = slice(128 * j, 128 * j + 128)
        block = r[:, 8 * j : 8 * j + 8, :].astype(F32)
        for f in range(2):
            part = jnp.concatenate([block[g, 4 * f : 4 * f + 4, :] for g in range(16)], 0).astype(BF)
            gs[f, :, lanes] = part
            for m in range(4):
                wide[m, 64 * f : 64 * f + 64, lanes] = part


def pack_space(ids, q, k, v, o0, o1, o2, o3, buf, turned, sem):
    x = ids[1]
    copies = fetch([(ref, buf.at[a]) for a, ref in enumerate((q, k, v))], sem)
    for a in range(3):
        copies[a].wait()
        turned[...] = buf[a].T.reshape(16, 64, 128)
        for m, o in enumerate((o0, o1, o2, o3)):
            for z in range(4):
                o[z, a, :, :] = turned[z * 4 + lax.rem(x + m, 4)]


def turn_space(ids, *refs):
    ins, outs = refs[:4], refs[4:]
    z = ids[0]
    for n in range(4):
        at = lax.rem(z + n, 4)
        for m in range(4):
            outs[n][m] = ins[m][at]


def space_forward(ids, s0, s1, s2, s3, heads, stats, o0, o1, o2, o3, buf, ot):
    z, x = ids[0], ids[1]
    for n, s in enumerate((s0, s1, s2, s3)):
        for m in range(4):
            buf[lax.rem(z + 4 - n, 4) * 4 + lax.rem(x + 4 - m, 4)] = s[m]
    for a in range(3):
        for f in range(2):
            heads[a, f] = jnp.concatenate(
                [buf[i, a, :, 64 * f : 64 * f + 64] for i in range(16)], 1
            )
    for f in range(2):
        score = dot(heads[1, f].T, heads[0, f] * jnp.asarray(SCALING, BF), ((1,), (0,)))
        largest = jnp.max(score, axis=0, keepdims=True)
        e = jnp.exp(score - largest)
        inverse = 1.0 / jnp.sum(e, axis=0, keepdims=True)
        stats[f, 0:1, :] = largest
        stats[f, 1:2, :] = inverse
        result = dot(heads[2, f], (e * inverse).astype(BF), ((1,), (0,))).astype(BF)
        for n in range(4):
            ot[n, f] = result[:, 256 * n : 256 * n + 256]
    for n, o in enumerate((o0, o1, o2, o3)):
        at = lax.rem(z + n, 4)
        for f in range(2):
            o[:, 256 * f : 256 * f + 256] = ot[at, f]


def mix_grads(ids, g, own, other, m0, m1, m2, m3, buf):
    buf[ids[3]] = own[...]
    buf[1 - ids[3]] = other[...]
    for n, m in enumerate((m0, m1, m2, m3)):
        w = jnp.concatenate([buf[0, n], buf[1, n]], 1)
        for x in range(4):
            m[:, 128 * x : 128 * x + 128] = dot(w, g[x], ((1,), (1,))).astype(BF)


def weight_grads(ids, g, r0, r1, r2, r3, o, held, buf):
    z = ids[0]
    for n, r in enumerate((r0, r1, r2, r3)):
        held[n] = r[:, 512:1024]
    for n, r in enumerate((r0, r1, r2, r3)):
        buf[lax.rem(z + 4 - n, 4)] = r[:, 0:512]
    left = buf[...].reshape(256, 512)
    for d in range(4):
        lanes = slice(256 * d, 256 * d + 256)
        right = jnp.concatenate(
            [g[x, 64 * f : 64 * f + 64, lanes] for f in range(2) for x in range(4)], 0
        )
        total = dot(left, right, ((1,), (0,))).reshape(4, 16, 4, 256)
        for y in range(16):
            o[y, :, lanes] = jnp.concatenate([total[n, y] for n in range(4)], 0).astype(BF)


def space_backward(ids, heads, stats, m0, m1, m2, m3, gq, gk, gv, buf, got, ds_all, w_all):
    z = ids[0]
    for n, m in enumerate((m0, m1, m2, m3)):
        buf[lax.rem(z + n, 4)] = m[...]
    scale = jnp.asarray(SCALING, BF)
    for f in range(2):
        got[...] = jnp.concatenate(
            [buf[n, :, 128 * x + 64 * f : 128 * x + 64 * f + 64] for n in range(4) for x in range(4)], 1
        )
        q, k = heads[0, f] * scale, heads[1, f]
        weight = jnp.exp(dot(k.T, q, ((1,), (0,))) - stats[f, 0:1, :]) * stats[f, 1:2, :]
        prob = dot(heads[2, f].T, got[...], ((1,), (0,)))
        delta = jnp.sum(weight * prob, axis=0, keepdims=True)
        ds_all[...] = (weight * (prob - delta)).astype(BF)
        w_all[...] = weight.astype(BF)
        gq[f] = dot(k * scale, ds_all[...], ((1,), (0,))).astype(BF)
        gk[f] = dot(ds_all[...], q.T, ((1,), (0,))).T.astype(BF)
        gv[f] = dot(w_all[...], got[...].T, ((1,), (0,))).T.astype(BF)


def add_up(r, o):
    total = r[0].astype(F32)
    for i in range(1, 16):
        total = total + r[i].astype(F32)
    for i in range(8):
        o[i] = total[2 * i : 2 * i + 2]


def shift(value, axis, by):
    return lax.ppermute(value, axis, [(i, (i + by) % 4) for i in range(4)])


def body(space_query, space_key, space_value, time_query, time_key, stream, cotangent, mix_weight):
    ids = jnp.stack([lax.axis_index(a) for a in ("z", "x", "f", "c")]).astype(jnp.int32)

    packed = call(
        pack_time,
        [((16, 272, 128), BF)],
        [t.reshape(2, 64, 1024) for t in (time_query, time_key, stream, cotangent)] + [mix_weight],
        specs=[HBM] * 4 + [VM],
        scratch=[
            pltpu.VMEM((4, 2, 64, 1024), BF),
            pltpu.VMEM((16, 272, 128), BF),
            pltpu.SemaphoreType.DMA((32,)),
            pltpu.SemaphoreType.DMA((4,)),
        ],
        places=[HBM],
        moved=2 << 20,
        name="pack_time",
        limit=WHOLE,
    )[0]
    frames = lax.all_to_all(packed, TM, 0, 0, tiled=True)

    part = ((4, 3, 64, 128), BF)
    sent = call(
        pack_space,
        [part] * 4,
        [ids] + [t.reshape(128, 1024) for t in (space_query, space_key, space_value)],
        specs=[SM] + [HBM] * 3,
        scratch=[
            pltpu.VMEM((3, 128, 1024), BF),
            pltpu.VMEM((16, 64, 128), BF),
            pltpu.SemaphoreType.DMA((3,)),
        ],
        moved=1536 << 10,
        name="pack_space",
        after=[packed],
    )
    along_x = [sent[0]] + [shift(sent[m], "x", m) for m in (1, 2, 3)]
    turned = call(
        turn_space, [part] * 4, [ids] + along_x, specs=[SM] + [VM] * 4, moved=1536 << 10, name="turn_space"
    )
    along_z = [turned[0]] + [shift(turned[n], "z", n) for n in (1, 2, 3)]

    grad_frames, own_rows = call(
        time_stream,
        [((16, 64, 128), BF), ((32, 512), BF)],
        [ids, frames],
        specs=[SM, VM],
        flops=1 << 30,
        moved=2 << 20,
        name="time_stream",
        after=[turned[0]],
    )
    back = lax.all_to_all(grad_frames, TM, 0, 0, tiled=True)
    other_rows = lax.ppermute(own_rows, "f", [(0, 1), (1, 0)])

    heads, stats, *outputs = call(
        space_forward,
        [((3, 2, 64, 1024), BF), ((2, 2, 1024), F32)] + [((64, 512), BF)] * 4,
        [ids] + along_z,
        specs=[SM] + [VM] * 4,
        scratch=[pltpu.VMEM((16, 3, 64, 128), BF), pltpu.VMEM((4, 2, 64, 256), BF)],
        flops=4 << 30,
        moved=2 << 20,
        name="space_forward",
        limit=FRAME,
    )

    grad_stream, wide, *outputs = call(
        unpack_stream,
        [((2, 64, 1024), BF), ((4, 128, 1024), BF)] + [((64, 1024), BF)] * 4,
        [ids, back, own_rows, other_rows] + outputs,
        specs=[SM] + [VM] * 7,
        moved=1536 << 10,
        name="unpack_stream",
    )
    gathered = lax.all_to_all(wide, "x", 0, 0, tiled=True)
    outputs = [outputs[0]] + [shift(outputs[n], "z", n) for n in (1, 2, 3)]

    grad_time_query, grad_time_key, token = call(
        time_grads,
        [((32, 4, 1024), BF)] * 2 + [((8, 128), F32)],
        [frames],
        flops=1 << 30,
        moved=2 << 20,
        name="time_grads",
        after=[stats],
    )
    partial, own_lanes = call(
        weight_grads,
        [((16, 16, 1024), BF), ((4, 64, 512), BF)],
        [ids, gathered] + outputs,
        specs=[SM] + [VM] * 5,
        scratch=[pltpu.VMEM((4, 64, 512), BF)],
        flops=1 << 28,
        moved=2 << 20,
        name="weight_grads",
        after=[token],
    )
    other_lanes = lax.ppermute(own_lanes, "c", [(0, 1), (1, 0)])
    spread = lax.all_to_all(partial, TM, 0, 0, tiled=True)
    mixed = call(
        mix_grads,
        [((64, 512), BF)] * 4,
        [ids, gathered, own_lanes, other_lanes],
        specs=[SM] + [VM] * 3,
        scratch=[pltpu.VMEM((2, 4, 64, 512), BF)],
        flops=1 << 28,
        moved=2 << 20,
        name="mix_grads",
    )
    mixed = [mixed[0]] + [shift(mixed[n], "z", -n) for n in (1, 2, 3)]

    summed = call(add_up, [((8, 2, 1024), F32)], [spread], moved=1 << 19, name="add_up", after=mixed[:1])[0]
    last = lax.all_to_all(summed, ("z", "f"), 0, 0, tiled=True)
    grads = call(
        space_backward,
        [((2, 64, 1024), BF)] * 3,
        [ids, heads, stats] + mixed,
        specs=[SM] + [VM] * 6,
        scratch=[
            pltpu.VMEM((4, 64, 512), BF),
            pltpu.VMEM((64, 1024), BF),
            pltpu.VMEM((1024, 1024), BF),
            pltpu.VMEM((1024, 1024), BF),
        ],
        flops=8 << 30,
        moved=4 << 20,
        name="space_backward",
        limit=FRAME,
        after=[summed],
    )
    grad_mix_weight = jnp.sum(last, axis=0)

    time_shape = (1, 32, 4, 1024)
    return (
        *(g.transpose(0, 2, 1).reshape(1, 2, 1024, 64) for g in grads),
        grad_time_query.reshape(time_shape),
        grad_time_key.reshape(time_shape),
        grad_stream.reshape(1, 2, 64, 1024),
        grad_mix_weight,
    )


def solution(mesh):
    fine = Mesh(mesh.devices.reshape(4, 4, 8, 2, 2), ("z", "x", "y", "c", "f"))
    tokens = P("f", TM, ("z", "x"), None)
    feature = P("f", TM, None, ("z", "x"))
    time = P("f", None, ("z", "x", "y", "c"), None)
    rows = P(("z", "x", "y", "c", "f"), None)
    return jax.shard_map(
        body,
        mesh=fine,
        in_specs=(tokens,) * 7 + (rows,),
        out_specs=(feature,) * 3 + (time,) * 2 + (tokens, rows),
        check_vma=False,
    )
```

```python
import jax
import jax.numpy as jnp
from jax import lax
from jax.experimental import pallas as pl
from jax.experimental.pallas import tpu as pltpu
from jax.sharding import Mesh, PartitionSpec as P

HD = 64
SCALING = HD ** (-0.5)
TM = ("y", "c")
BF = jnp.bfloat16
F32 = jnp.float32
LIMIT = 16 * 1024 * 1024
FRAME = 32 * 1024 * 1024
WHOLE = 60 * 1024 * 1024
VM = pl.BlockSpec(memory_space=pltpu.VMEM)
SM = pl.BlockSpec(memory_space=pltpu.SMEM)
ANY = pl.BlockSpec(memory_space=pl.ANY)
HBM = pl.BlockSpec(memory_space=pltpu.HBM)


def call(kernel, outs, ins, specs=None, scratch=(), flops=0, moved=0, name=None, after=(), limit=LIMIT, places=None):
    shapes = [jax.ShapeDtypeStruct(s, d) for s, d in outs]
    specs = specs or [VM] * len(ins)
    first, count = len(ins), len(after)

    def run(*refs):
        kernel(*refs[:first], *refs[first + count :])

    return pl.pallas_call(
        run,
        out_shape=shapes,
        in_specs=list(specs) + [ANY] * count,
        out_specs=places or [VM] * len(shapes),
        scratch_shapes=list(scratch),
        compiler_params=pltpu.CompilerParams(vmem_limit_bytes=limit),
        cost_estimate=pl.CostEstimate(flops=flops, bytes_accessed=moved, transcendentals=0),
        name=name,
    )(*ins, *after)


def fetch(pairs, sem):
    copies = [pltpu.make_async_copy(a, b, sem.at[i]) for i, (a, b) in enumerate(pairs)]
    for copy in copies:
        copy.start()
    return copies


def dot(a, b, dims):
    return lax.dot_general(a, b, (dims, ((), ())), preferred_element_type=F32)


def pack_time(tq, tk, st, ct, w, o, buf, stage, sem, out_sem):
    copies = [
        pltpu.make_async_copy(
            ref.at[f, pl.ds(16 * h, 16)], buf.at[a, f, pl.ds(16 * h, 16)], sem.at[8 * h + 2 * a + f]
        )
        for h in range(4)
        for a, ref in enumerate((tq, tk, st, ct))
        for f in range(2)
    ]
    for copy in copies:
        copy.start()
    own = w[...].astype(F32)
    own = jnp.concatenate([own[:, 128 * j : 128 * j + 128] for j in range(8)], 0).astype(BF)
    for g in range(16):
        stage[g, 256:272, :] = own
    results = []
    for h in range(4):
        for copy in copies[8 * h : 8 * h + 8]:
            copy.wait()
        for j in range(8):
            lanes = slice(128 * j, 128 * j + 128)
            wide = [[buf[a, f, 16 * h : 16 * h + 16, lanes].astype(F32) for f in range(2)] for a in range(4)]
            for g in range(4):
                rows = slice(4 * g, 4 * g + 4)
                block = jnp.concatenate([wide[a][f][rows] for a in range(4) for f in range(2)], 0)
                stage[4 * h + g, 32 * j : 32 * j + 32, :] = block.astype(BF)
        results.append(
            pltpu.make_async_copy(stage.at[pl.ds(4 * h, 4)], o.at[pl.ds(4 * h, 4)], out_sem.at[h])
        )
        results[-1].start()
    for copy in results:
        copy.wait()


def time_heads(r):
    row = lax.broadcasted_iota(jnp.int32, (128, 128), 0)
    col = lax.broadcasted_iota(jnp.int32, (128, 128), 1)
    allowed = ((row & 3) == (col & 3)) & (row <= col)
    bias = jnp.where(allowed, 0.0, -jnp.inf).astype(F32)
    zero = jnp.zeros((128, 128), BF)
    scale = jnp.asarray(SCALING, BF)
    cots, heads = [], []
    for j in range(8):
        block = r[:, 32 * j : 32 * j + 32, :].astype(F32)
        q, k, v, cot = (block[:, 8 * a : 8 * a + 8, :].reshape(128, 128) for a in range(4))
        cots.append(cot)
        q, k, v, g = (t.astype(BF) for t in (q, k, v, cot))
        for own in (col < 64, col >= 64):
            qh, kh, gh = (jnp.where(own, t, zero) for t in (q, k, g))
            heads.append((qh, k, kh, v, gh))
    scores = [dot(k, qh * scale, ((1,), (1,))) + bias for qh, k, _, _, _ in heads]
    exps = [jnp.exp(s - jnp.max(s, axis=0, keepdims=True)) for s in scores]
    weights = [e * (1.0 / jnp.sum(e, axis=0, keepdims=True)) for e in exps]
    return cots, heads, weights


def time_stream(ids, r, gs, wo):
    cots, heads, weights = time_heads(r)
    parts = [dot(w.astype(BF), h[4], ((1,), (0,))) for w, h in zip(weights, heads)]
    for j in range(0, 8, 2):
        pair = [(cots[i] + (parts[2 * i] + parts[2 * i + 1])).reshape(16, 8, 128) for i in (j, j + 1)]
        gs[:, 8 * j : 8 * j + 16, :] = jnp.concatenate(pair, 1).astype(BF)
    rows = r[:, 256:272, :].astype(F32)
    rows = jnp.where(jnp.full((16, 8, 128), ids[3], jnp.int32) == 1, rows[:, 8:16], rows[:, 0:8])
    for j in range(4):
        wo[:, 128 * j : 128 * j + 128] = jnp.concatenate(
            [rows[g, 2 * j : 2 * j + 2, :] for g in range(16)], 0
        ).astype(BF)


def time_grads(r, gq, gk, token):
    token[...] = jnp.zeros((8, 128), F32)
    _, heads, weights = time_heads(r)
    probs = [dot(v, gh, ((1,), (1,))) for _, _, _, v, gh in heads]
    deltas = [jnp.sum(w * p, axis=0, keepdims=True) for w, p in zip(weights, probs)]
    ds = [(w * (p - d) * SCALING).astype(BF) for w, p, d in zip(weights, probs, deltas)]
    parts_k = [dot(d, h[0], ((1,), (0,))) for d, h in zip(ds, heads)]
    parts_q = [dot(d, h[2], ((0,), (0,))) for d, h in zip(ds, heads)]
    for j in range(8):
        lanes = slice(128 * j, 128 * j + 128)
        gq[:, :, lanes] = (parts_q[2 * j] + parts_q[2 * j + 1]).reshape(32, 4, 128).astype(BF)
        gk[:, :, lanes] = (parts_k[2 * j] + parts_k[2 * j + 1]).reshape(32, 4, 128).astype(BF)


def unpack_stream(ids, r, own, other, s0, s1, s2, s3, gs, wide, *outs):
    for s, o in zip((s0, s1, s2, s3), outs):
        o[:, 0:512] = s[...]
    swapped = jnp.full((32, 128), ids[2], jnp.int32) == 1
    for j in range(4):
        lanes = slice(128 * j, 128 * j + 128)
        mine, theirs = own[:, lanes].astype(F32), other[:, lanes].astype(F32)
        low = jnp.where(swapped, theirs, mine)
        high = jnp.where(swapped, mine, theirs)
        pieces = [t[2 * y : 2 * y + 2] for y in range(16) for t in (low, high)]
        rows = jnp.concatenate(pieces, 0).astype(BF)
        for o in outs:
            o[:, 512 + 128 * j : 640 + 128 * j] = rows
    for j in range(8):
        lanes = slice(128 * j, 128 * j + 128)
        block = r[:, 8 * j : 8 * j + 8, :].astype(F32)
        for f in range(2):
            part = jnp.concatenate([block[g, 4 * f : 4 * f + 4, :] for g in range(16)], 0).astype(BF)
            gs[f, :, lanes] = part
            for m in range(4):
                wide[m, 64 * f : 64 * f + 64, lanes] = part


def pack_space(ids, q, k, v, o0, o1, o2, o3, buf, turned, sem):
    x = ids[1]
    copies = fetch([(ref, buf.at[a]) for a, ref in enumerate((q, k, v))], sem)
    for a in range(3):
        copies[a].wait()
        turned[...] = buf[a].T.reshape(16, 64, 128)
        for m, o in enumerate((o0, o1, o2, o3)):
            for z in range(4):
                o[z, a, :, :] = turned[z * 4 + lax.rem(x + m, 4)]


def turn_space(ids, *refs):
    ins, outs = refs[:4], refs[4:]
    z = ids[0]
    for n in range(4):
        at = lax.rem(z + n, 4)
        for m in range(4):
            outs[n][m] = ins[m][at]


def space_forward(ids, s0, s1, s2, s3, heads, stats, o0, o1, o2, o3, buf, ot):
    z, x = ids[0], ids[1]
    for n, s in enumerate((s0, s1, s2, s3)):
        for m in range(4):
            buf[lax.rem(z + 4 - n, 4) * 4 + lax.rem(x + 4 - m, 4)] = s[m]
    for a in range(3):
        for f in range(2):
            heads[a, f] = jnp.concatenate(
                [buf[i, a, :, 64 * f : 64 * f + 64] for i in range(16)], 1
            )
    for f in range(2):
        score = dot(heads[1, f].T, heads[0, f] * jnp.asarray(SCALING, BF), ((1,), (0,)))
        largest = jnp.max(score, axis=0, keepdims=True)
        e = jnp.exp(score - largest)
        inverse = 1.0 / jnp.sum(e, axis=0, keepdims=True)
        stats[f, 0:1, :] = largest
        stats[f, 1:2, :] = inverse
        result = dot(heads[2, f], (e * inverse).astype(BF), ((1,), (0,))).astype(BF)
        for n in range(4):
            ot[n, f] = result[:, 256 * n : 256 * n + 256]
    for n, o in enumerate((o0, o1, o2, o3)):
        at = lax.rem(z + n, 4)
        for f in range(2):
            o[:, 256 * f : 256 * f + 256] = ot[at, f]


def mix_grads(ids, g, own, other, m0, m1, m2, m3, buf):
    for n in range(4):
        part = (slice(128 + 64 * (n // 2), 192 + 64 * (n // 2)), slice(512 * (n % 2), 512 * (n % 2) + 512))
        buf[ids[3], n] = own[part]
        buf[1 - ids[3], n] = other[part]
    for n, m in enumerate((m0, m1, m2, m3)):
        w = jnp.concatenate([buf[0, n], buf[1, n]], 1)
        for x in range(4):
            m[:, 128 * x : 128 * x + 128] = dot(w, g[x], ((1,), (1,))).astype(BF)


def weight_grads(ids, g, r0, r1, r2, r3, kept, sent, buf):
    z = ids[0]
    for n, r in enumerate((r0, r1, r2, r3)):
        sent[128 + 64 * (n // 2) : 192 + 64 * (n // 2), 512 * (n % 2) : 512 * (n % 2) + 512] = r[:, 512:1024]
        buf[lax.rem(z + 4 - n, 4)] = r[:, 0:512]
    left = buf[...].reshape(256, 512)
    second = jnp.full((16, 256), ids[3], jnp.int32) == 1
    for d in range(4):
        lanes = slice(256 * d, 256 * d + 256)
        right = jnp.concatenate(
            [g[x, 64 * f : 64 * f + 64, lanes] for f in range(2) for x in range(4)], 0
        )
        total = dot(left, right, ((1,), (0,))).reshape(4, 16, 4, 256)
        for y in range(8):
            v0, v1 = (jnp.concatenate([total[n, 2 * y + c] for n in range(4)], 0) for c in range(2))
            kept[16 * y : 16 * y + 16, lanes] = jnp.where(second, v1, v0)
            sent[16 * y : 16 * y + 16, lanes] = jnp.where(second, v0, v1).astype(BF)


def add_pair(kept, got, o, token):
    token[...] = jnp.zeros((8, 128), F32)
    o[...] = (kept[...] + got[0:128, :].astype(F32)).astype(BF).reshape(8, 16, 1024)


def space_backward(ids, heads, stats, m0, m1, m2, m3, gq, gk, gv, buf, got, ds_all, w_all):
    z = ids[0]
    for n, m in enumerate((m0, m1, m2, m3)):
        buf[lax.rem(z + n, 4)] = m[...]
    scale = jnp.asarray(SCALING, BF)
    for f in range(2):
        got[...] = jnp.concatenate(
            [buf[n, :, 128 * x + 64 * f : 128 * x + 64 * f + 64] for n in range(4) for x in range(4)], 1
        )
        q, k = heads[0, f] * scale, heads[1, f]
        weight = jnp.exp(dot(k.T, q, ((1,), (0,))) - stats[f, 0:1, :]) * stats[f, 1:2, :]
        prob = dot(heads[2, f].T, got[...], ((1,), (0,)))
        delta = jnp.sum(weight * prob, axis=0, keepdims=True)
        ds_all[...] = (weight * (prob - delta)).astype(BF)
        w_all[...] = weight.astype(BF)
        gq[f] = dot(k * scale, ds_all[...], ((1,), (0,))).astype(BF)
        gk[f] = dot(ds_all[...], q.T, ((1,), (0,))).T.astype(BF)
        gv[f] = dot(w_all[...], got[...].T, ((1,), (0,))).T.astype(BF)


def add_up(r, o):
    total = r[0].astype(F32)
    for i in range(1, 8):
        total = total + r[i].astype(F32)
    for i in range(8):
        o[i] = total[2 * i : 2 * i + 2]


def shift(value, axis, by):
    return lax.ppermute(value, axis, [(i, (i + by) % 4) for i in range(4)])


def body(space_query, space_key, space_value, time_query, time_key, stream, cotangent, mix_weight):
    ids = jnp.stack([lax.axis_index(a) for a in ("z", "x", "f", "c")]).astype(jnp.int32)

    packed = call(
        pack_time,
        [((16, 272, 128), BF)],
        [t.reshape(2, 64, 1024) for t in (time_query, time_key, stream, cotangent)] + [mix_weight],
        specs=[HBM] * 4 + [VM],
        scratch=[
            pltpu.VMEM((4, 2, 64, 1024), BF),
            pltpu.VMEM((16, 272, 128), BF),
            pltpu.SemaphoreType.DMA((32,)),
            pltpu.SemaphoreType.DMA((4,)),
        ],
        places=[HBM],
        moved=2 << 20,
        name="pack_time",
        limit=WHOLE,
    )[0]
    frames = lax.all_to_all(packed, TM, 0, 0, tiled=True)

    part = ((4, 3, 64, 128), BF)
    sent = call(
        pack_space,
        [part] * 4,
        [ids] + [t.reshape(128, 1024) for t in (space_query, space_key, space_value)],
        specs=[SM] + [HBM] * 3,
        scratch=[
            pltpu.VMEM((3, 128, 1024), BF),
            pltpu.VMEM((16, 64, 128), BF),
            pltpu.SemaphoreType.DMA((3,)),
        ],
        moved=1536 << 10,
        name="pack_space",
        after=[packed],
    )
    along_x = [sent[0]] + [shift(sent[m], "x", m) for m in (1, 2, 3)]
    turned = call(
        turn_space, [part] * 4, [ids] + along_x, specs=[SM] + [VM] * 4, moved=1536 << 10, name="turn_space"
    )
    along_z = [turned[0]] + [shift(turned[n], "z", n) for n in (1, 2, 3)]

    grad_frames, own_rows = call(
        time_stream,
        [((16, 64, 128), BF), ((32, 512), BF)],
        [ids, frames],
        specs=[SM, VM],
        flops=1 << 30,
        moved=2 << 20,
        name="time_stream",
        after=[turned[0]],
    )
    back = lax.all_to_all(grad_frames, TM, 0, 0, tiled=True)
    other_rows = lax.ppermute(own_rows, "f", [(0, 1), (1, 0)])

    heads, stats, *outputs = call(
        space_forward,
        [((3, 2, 64, 1024), BF), ((2, 2, 1024), F32)] + [((64, 512), BF)] * 4,
        [ids] + along_z,
        specs=[SM] + [VM] * 4,
        scratch=[pltpu.VMEM((16, 3, 64, 128), BF), pltpu.VMEM((4, 2, 64, 256), BF)],
        flops=4 << 30,
        moved=2 << 20,
        name="space_forward",
        limit=FRAME,
    )

    grad_stream, wide, *outputs = call(
        unpack_stream,
        [((2, 64, 1024), BF), ((4, 128, 1024), BF)] + [((64, 1024), BF)] * 4,
        [ids, back, own_rows, other_rows] + outputs,
        specs=[SM] + [VM] * 7,
        moved=1536 << 10,
        name="unpack_stream",
    )
    gathered = lax.all_to_all(wide, "x", 0, 0, tiled=True)
    outputs = [outputs[0]] + [shift(outputs[n], "z", n) for n in (1, 2, 3)]

    grad_time_query, grad_time_key, token = call(
        time_grads,
        [((32, 4, 1024), BF)] * 2 + [((8, 128), F32)],
        [frames],
        flops=1 << 30,
        moved=2 << 20,
        name="time_grads",
        after=[stats],
    )
    partial, sent_pair = call(
        weight_grads,
        [((128, 1024), F32), ((256, 1024), BF)],
        [ids, gathered] + outputs,
        specs=[SM] + [VM] * 5,
        scratch=[pltpu.VMEM((4, 64, 512), BF)],
        flops=1 << 28,
        moved=2 << 20,
        name="weight_grads",
        after=[token],
    )
    got_pair = lax.ppermute(sent_pair, "c", [(0, 1), (1, 0)])
    partial, token = call(
        add_pair,
        [((8, 16, 1024), BF), ((8, 128), F32)],
        [partial, got_pair],
        moved=1 << 20,
        name="add_pair",
    )
    spread = lax.all_to_all(partial, "y", 0, 0, tiled=True)
    mixed = call(
        mix_grads,
        [((64, 512), BF)] * 4,
        [ids, gathered, sent_pair, got_pair],
        specs=[SM] + [VM] * 3,
        scratch=[pltpu.VMEM((2, 4, 64, 512), BF)],
        flops=1 << 28,
        moved=2 << 20,
        name="mix_grads",
        after=[token],
    )
    mixed = [mixed[0]] + [shift(mixed[n], "z", -n) for n in (1, 2, 3)]

    summed = call(add_up, [((8, 2, 1024), F32)], [spread], moved=1 << 19, name="add_up", after=mixed[:1])[0]
    last = lax.all_to_all(summed, ("z", "f"), 0, 0, tiled=True)
    grads = call(
        space_backward,
        [((2, 64, 1024), BF)] * 3,
        [ids, heads, stats] + mixed,
        specs=[SM] + [VM] * 6,
        scratch=[
            pltpu.VMEM((4, 64, 512), BF),
            pltpu.VMEM((64, 1024), BF),
            pltpu.VMEM((1024, 1024), BF),
            pltpu.VMEM((1024, 1024), BF),
        ],
        flops=8 << 30,
        moved=4 << 20,
        name="space_backward",
        limit=FRAME,
        after=[summed],
    )
    grad_mix_weight = jnp.sum(last, axis=0)

    time_shape = (1, 32, 4, 1024)
    return (
        *(g.transpose(0, 2, 1).reshape(1, 2, 1024, 64) for g in grads),
        grad_time_query.reshape(time_shape),
        grad_time_key.reshape(time_shape),
        grad_stream.reshape(1, 2, 64, 1024),
        grad_mix_weight,
    )


def solution(mesh):
    fine = Mesh(mesh.devices.reshape(4, 4, 8, 2, 2), ("z", "x", "y", "c", "f"))
    tokens = P("f", TM, ("z", "x"), None)
    feature = P("f", TM, None, ("z", "x"))
    time = P("f", None, ("z", "x", "y", "c"), None)
    rows = P(("z", "x", "y", "c", "f"), None)
    return jax.shard_map(
        body,
        mesh=fine,
        in_specs=(tokens,) * 7 + (rows,),
        out_specs=(feature,) * 3 + (time,) * 2 + (tokens, rows),
        check_vma=False,
    )
```
